32 devices in a mesh: row: 4 (over y, x), col: 8 (over z, core).
Axes of the slice: x: 2, y: 2, z: 4, core: 2. Of those that a mesh axis runs over, the one named last changes fastest.
Arguments:
- density: float32 [32, 7, 128, 128], P(('row', 'col')), as said below
- pattern: int32 [32, 12], P(('row', 'col')), may hold values from 0 to 31, as said below
Outputs:
- purified: float32 [32, 7, 128, 128], P(('row', 'col'))
The draws below stay inside these ranges and needn't reach their ends.
Inputs may be any that keep to these rules, and one draw needn't show every extreme that they name: `pattern`: row I lists the block columns (I + o) mod 32 for o = -6..6 in rising order of o, all but one o; the omitted o is nonzero and of magnitude 3 or less, and row (I + o) mod 32 omits -o. density[I, 0] is symmetric, and density[I, t] is zero where (I + t) mod 32 is not listed in row I of pattern.
All inputs are finite; a program needn't handle non-finite values.
Results may differ from the reference program's by a relative error of at most 0.0001.
Values sent between devices are 32-bit elements; how exact they have to be, the bound alone decides.
A program may use at most 64 MiB of HBM per device.

```python
import jax
import jax.numpy as jnp
from jax import lax

BLOCK = 128
REACH = 6
PER_ROW = 12
BLOCKS = 32


def partner_offsets(key):
    picks = jax.random.randint(jax.random.fold_in(key, 11), (BLOCKS // 4,), 0, 3)
    table = jnp.array([[1, -1, 1, -1], [2, 2, -2, -2], [3, 1, -1, -3]], jnp.int32)
    return table[picks].reshape(BLOCKS).astype(jnp.int32)


def draw_pattern(key, part):
    partner = partner_offsets(key)
    removed = partner + REACH
    kept = jnp.arange(PER_ROW, dtype=jnp.int32)[None, :]
    index = kept + (kept >= removed[:, None]).astype(jnp.int32)
    offsets = index - REACH
    listed = jnp.arange(BLOCKS, dtype=jnp.int32)[:, None]
    return ((listed + offsets + BLOCKS) % BLOCKS).astype(jnp.int32)


def draw_density(key, part):
    partner = partner_offsets(key)
    value_key = jax.random.fold_in(key, 23)
    shape = (BLOCKS, REACH + 1, BLOCK, BLOCK)
    spread = 1.5 / (PER_ROW * BLOCK) ** 0.5
    raw = jax.random.normal(value_key, shape, jnp.float32)
    diagonal = (raw[:, 0] + jnp.swapaxes(raw[:, 0], 1, 2)) * 0.5
    beside = raw[:, 1:] * 0.70710678
    band = jnp.concatenate([diagonal[:, None], beside], axis=1)
    keep = (jnp.arange(REACH + 1, dtype=jnp.int32)[None, :] != partner[:, None]).astype(jnp.float32)
    return (band * spread * keep[:, :, None, None]).astype(jnp.float32)


def setup_inputs(seed: int = 0) -> dict:
    arg_keys = jax.random.split(jax.random.key(seed), 3)
    density = draw_density(jax.random.fold_in(arg_keys[2], 71), 0)
    pattern = draw_pattern(jax.random.fold_in(arg_keys[2], 71), 0)
    return dict(density=density, pattern=pattern)


def upper_block(band, offset, width):
    return jnp.roll(band[:, width], -offset, axis=0)


def block_at(band, inner, target):
    if target >= inner:
        return upper_block(band, inner, target - inner)
    return jnp.swapaxes(upper_block(band, target, inner - target), 1, 2)


def band_product(band_left, band_right):
    results = []
    for target in range(REACH + 1):
        total = jnp.zeros((BLOCKS, BLOCK, BLOCK), jnp.float32)
        for inner in range(target - REACH, REACH + 1):
            left = block_at(band_left, 0, inner).astype(jnp.float32)
            right = block_at(band_right, inner, target).astype(jnp.float32)
            total = total + jnp.einsum("zab,zbc->zac", left, right, precision=lax.Precision.HIGHEST, preferred_element_type=jnp.float32)
        results.append(total)
    return jnp.stack(results, axis=1)


def reference(density, pattern):
    listed = jnp.arange(BLOCKS, dtype=jnp.int32)
    columns = (listed[:, None] + jnp.arange(REACH + 1, dtype=jnp.int32)[None, :]) % BLOCKS
    flags = jnp.any(pattern[:, None, :] == columns[:, :, None], axis=2).astype(jnp.float32)[:, :, None, None]
    square = flags * band_product(density, density)
    cube = flags * band_product(density, square)
    return 3.0 * square - 2.0 * cube
```

```python
import functools

import jax
import jax.numpy as jnp
from jax import lax
from jax.experimental import pallas as pl
from jax.experimental.pallas import tpu as pltpu
from jax.sharding import PartitionSpec as P

REACH = 6
SLOTS = REACH + 1
MESH = pl.DeviceIdType.MESH
NN = (((1,), (0,)), ((), ()))
NT = (((1,), (1,)), ((), ()))


def split(value):
    high = value.astype(jnp.bfloat16)
    low = (value - high.astype(jnp.float32)).astype(jnp.bfloat16)
    return high, low


def side(blocks):
    return blocks[0] if len(blocks) == 1 else jnp.concatenate(blocks, axis=1)


def times(left, right):
    lh, ll = left
    rh, rl = right
    return lax.dot_general(
        jnp.concatenate([lh, ll, lh], axis=1),
        jnp.concatenate([rh, rh, rl], axis=0),
        NN,
        preferred_element_type=jnp.float32,
    )


def times_transposed(left, right):
    lh, ll = left
    rh, rl = right
    return lax.dot_general(
        jnp.concatenate([lh, ll, lh], axis=1),
        jnp.concatenate([rh, rh, rl], axis=1),
        NT,
        preferred_element_type=jnp.float32,
    )


def ready(slot):
    return max(slot, REACH - slot)


def kernel(
    rows,
    cols,
    own,
    pattern,
    out,
    up_p,
    down_p,
    up_s,
    down_s,
    square,
    cube,
    own_high,
    own_low,
    left_high,
    left_low,
    p_send,
    p_recv,
    s_send,
    s_recv,
):
    total = rows * cols
    me = lax.axis_index("row") * cols + lax.axis_index("col")

    def device(index):
        return (index // cols, lax.rem(index, cols))

    right = device(lax.rem(me + 1, total))
    left = device(lax.rem(me + total - 1, total))

    def p_right(hop):
        slots = pl.ds(hop, SLOTS - hop)
        return pltpu.make_async_remote_copy(
            src_ref=own.at[0, slots] if hop == 1 else up_p.at[hop - 2, slots],
            dst_ref=up_p.at[hop - 1, slots],
            send_sem=p_send.at[0, hop - 1],
            recv_sem=p_recv.at[0, hop - 1],
            device_id=right,
            device_id_type=MESH,
        )

    def p_left(hop):
        slots = pl.ds(0, SLOTS - hop)
        return pltpu.make_async_remote_copy(
            src_ref=own.at[0, slots] if hop == 1 else down_p.at[hop - 2, slots],
            dst_ref=down_p.at[hop - 1, slots],
            send_sem=p_send.at[1, hop - 1],
            recv_sem=p_recv.at[1, hop - 1],
            device_id=left,
            device_id_type=MESH,
        )

    def s_right(hop, slot):
        return pltpu.make_async_remote_copy(
            src_ref=square.at[slot] if hop == 1 else up_s.at[hop - 2, slot],
            dst_ref=up_s.at[hop - 1, slot],
            send_sem=s_send.at[0, hop - 1, slot],
            recv_sem=s_recv.at[0, hop - 1, slot],
            device_id=right,
            device_id_type=MESH,
        )

    def s_left(hop, slot):
        return pltpu.make_async_remote_copy(
            src_ref=square.at[slot] if hop == 1 else down_s.at[hop - 2, slot],
            dst_ref=down_s.at[hop - 1, slot],
            send_sem=s_send.at[1, hop - 1, slot],
            recv_sem=s_recv.at[1, hop - 1, slot],
            device_id=left,
            device_id_type=MESH,
        )

    barrier = pltpu.get_barrier_semaphore()
    for neighbour in (left, right):
        pl.semaphore_signal(barrier, inc=1, device_id=neighbour, device_id_type=MESH)
    pl.semaphore_wait(barrier, 2)

    p_right(1).start()
    p_left(1).start()

    flags = []
    for slot in range(SLOTS):
        column = lax.rem(me + slot, total)
        listed = jnp.int32(0)
        for place in range(pattern.shape[1]):
            listed = listed | (pattern[0, place] == column).astype(jnp.int32)
        flags.append(listed.astype(jnp.float32))

    for slot in range(SLOTS):
        high, low = split(own[0, slot])
        own_high[slot] = high
        own_low[slot] = low

    def own_pair(first, last):
        return (
            side([own_high[i] for i in range(first, last)]),
            side([own_low[i] for i in range(first, last)]),
        )

    def add(target, first, value):
        for i in range(value.shape[1] // 128):
            target[first + i] += value[:, i * 128 : (i + 1) * 128]

    def local(target, band_high_low):
        band = band_high_low
        value = times(own_pair(0, 1), band)
        for i in range(SLOTS):
            target[i] = value[:, i * 128 : (i + 1) * 128]
        rest = (band[0][:, 128:], band[1][:, 128:])
        target[0] += times_transposed(own_pair(1, SLOTS), rest)

    def from_up(target, buffer, hop):
        value = split(side([buffer[hop - 1, i] for i in range(hop, SLOTS)]))
        add(target, 0, times((left_high[hop - 1], left_low[hop - 1]), value))

    def from_down(target, buffer, hop):
        value = split(side([buffer[hop - 1, i] for i in range(SLOTS - hop)]))
        add(target, hop, times(own_pair(hop, hop + 1), value))
        if hop < REACH:
            rest = (value[0][:, 128:], value[1][:, 128:])
            add(target, hop, times_transposed(own_pair(hop + 1, SLOTS), rest))

    local(square, own_pair(0, SLOTS))

    for step in range(1, 2 * REACH + 1):
        if step <= REACH:
            p_right(step).wait_recv()
            if step < REACH:
                p_right(step + 1).start()
            p_left(step).wait_recv()
            if step < REACH:
                p_left(step + 1).start()
        for hop in range(REACH, 0, -1):
            for slot in range(SLOTS):
                if ready(slot) + hop != step:
                    continue
                if hop <= slot:
                    s_right(hop, slot).wait_recv()
                    if hop < slot:
                        s_right(hop + 1, slot).start()
                if hop <= REACH - slot:
                    s_left(hop, slot).wait_recv()
                    if hop < REACH - slot:
                        s_left(hop + 1, slot).start()
        if step <= REACH:
            high, low = split(up_p[step - 1, step].T)
            left_high[step - 1] = high
            left_low[step - 1] = low
            from_up(square, up_p, step)
            from_down(square, down_p, step)
            for slot in range(SLOTS):
                if ready(slot) == step:
                    square[slot] = square[slot] * flags[slot]
                    if slot >= 1:
                        s_right(1, slot).start()
                    if slot < REACH:
                        s_left(1, slot).start()
            if step == REACH:
                local(cube, split(side([square[i] for i in range(SLOTS)])))
        else:
            from_up(cube, up_s, step - REACH)
            from_down(cube, down_s, step - REACH)

    for slot in range(SLOTS):
        out[0, slot] = 3.0 * square[slot] - (2.0 * flags[slot]) * cube[slot]

    for hop in range(1, REACH + 1):
        p_right(hop).wait_send()
        p_left(hop).wait_send()
        for slot in range(SLOTS):
            if hop <= slot:
                s_right(hop, slot).wait_send()
            if hop <= REACH - slot:
                s_left(hop, slot).wait_send()


def solution(mesh):
    rows, cols = mesh.shape["row"], mesh.shape["col"]

    def on_device(density, pattern):
        halo = pltpu.VMEM((REACH, SLOTS, 128, 128), jnp.float32)
        band = pltpu.VMEM((SLOTS, 128, 128), jnp.float32)
        return pl.pallas_call(
            functools.partial(kernel, rows, cols),
            out_shape=jax.ShapeDtypeStruct(density.shape, jnp.float32),
            in_specs=[
                pl.BlockSpec(memory_space=pltpu.VMEM),
                pl.BlockSpec(memory_space=pltpu.SMEM),
            ],
            out_specs=pl.BlockSpec(memory_space=pltpu.VMEM),
            scratch_shapes=[
                halo,
                halo,
                halo,
                halo,
                band,
                band,
                pltpu.VMEM((SLOTS, 128, 128), jnp.bfloat16),
                pltpu.VMEM((SLOTS, 128, 128), jnp.bfloat16),
                pltpu.VMEM((REACH, 128, 128), jnp.bfloat16),
                pltpu.VMEM((REACH, 128, 128), jnp.bfloat16),
                pltpu.SemaphoreType.DMA((2, REACH)),
                pltpu.SemaphoreType.DMA((2, REACH)),
                pltpu.SemaphoreType.DMA((2, REACH, SLOTS)),
                pltpu.SemaphoreType.DMA((2, REACH, SLOTS)),
            ],
            compiler_params=pltpu.CompilerParams(
                collective_id=0, has_side_effects=True, vmem_limit_bytes=40 * 1024 * 1024
            ),
            cost_estimate=pl.CostEstimate(
                flops=140 * 2 * 128**3, bytes_accessed=14 * 4 * 128**2, transcendentals=0
            ),
        )(density, pattern)

    return jax.shard_map(
        on_device,
        mesh=mesh,
        in_specs=(P(("row", "col"), None, None, None), P(("row", "col"), None)),
        out_specs=P(("row", "col"), None, None, None),
        check_vma=False,
    )
```

```python
import functools

import jax
import jax.numpy as jnp
from jax import lax
from jax.experimental import pallas as pl
from jax.experimental.pallas import tpu as pltpu
from jax.sharding import PartitionSpec as P

REACH = 6
SLOTS = REACH + 1
MESH = pl.DeviceIdType.MESH
FAR_FIRST = (6, 0, 5, 1, 4, 2, 3)
NN = (((1,), (0,)), ((), ()))
NT = (((1,), (1,)), ((), ()))


def split(value):
    high = value.astype(jnp.bfloat16)
    low = (value - high.astype(jnp.float32)).astype(jnp.bfloat16)
    return high, low


def side(blocks):
    return blocks[0] if len(blocks) == 1 else jnp.concatenate(blocks, axis=1)


def times(left, right):
    lh, ll = left
    rh, rl = right
    return lax.dot_general(
        jnp.concatenate([lh, ll, lh], axis=1),
        jnp.concatenate([rh, rh, rl], axis=0),
        NN,
        preferred_element_type=jnp.float32,
    )


def times_transposed(left, right):
    lh, ll = left
    rh, rl = right
    return lax.dot_general(
        jnp.concatenate([lh, ll, lh], axis=1),
        jnp.concatenate([rh, rh, rl], axis=1),
        NT,
        preferred_element_type=jnp.float32,
    )


def ready(slot):
    return max(slot, REACH - slot)


CYCLE = (0, 8, 9, 1, 5, 6, 7, 3, 2, 10, 11, 15, 14, 13, 12, 4)


def look_up(table, index):
    value = jnp.int32(0)
    for place, entry in enumerate(table):
        value = value + jnp.where(index == place, entry, 0)
    return value


def cycle_device(rows, cols, index):
    if (rows, cols) == (4, 8):
        index = 2 * look_up(CYCLE, index // 2) + lax.rem(index, 2)
    return index // cols, lax.rem(index, cols)


def cycle_row(rows, cols, line, place):
    index = line * cols + place
    if (rows, cols) == (4, 8):
        chips = [CYCLE.index(chip) for chip in range(len(CYCLE))]
        index = 2 * look_up(chips, index // 2) + lax.rem(index, 2)
    return index


def kernel(
    rows,
    cols,
    given,
    pattern,
    out,
    own,
    result,
    given_flags,
    flags,
    up_p,
    down_p,
    up_s,
    down_s,
    square,
    cube,
    own_high,
    own_low,
    left_high,
    left_low,
    p_send,
    p_recv,
    s_send,
    s_recv,
    swap_send,
    swap_recv,
):
    total = rows * cols
    line, place = lax.axis_index("row"), lax.axis_index("col")
    given_row = line * cols + place
    me = cycle_row(rows, cols, line, place)

    def device(index):
        return cycle_device(rows, cols, index)

    right = device(lax.rem(me + 1, total))
    left = device(lax.rem(me + total - 1, total))
    worker = device(given_row)
    owner = (me // cols, lax.rem(me, cols))
    moved = me != given_row

    def move(source, target, kind, index, to):
        return pltpu.make_async_remote_copy(
            src_ref=source,
            dst_ref=target,
            send_sem=swap_send.at[kind, index],
            recv_sem=swap_recv.at[kind, index],
            device_id=to,
            device_id_type=MESH,
        )

    def move_in(slot):
        return move(given.at[0, slot], own.at[slot], 0, slot, worker)

    def move_flags():
        return move(given_flags, flags, 0, SLOTS, worker)

    def move_out(slot):
        return move(result.at[slot], out.at[0, slot], 1, slot, owner)

    def p_right(hop, slot):
        return pltpu.make_async_remote_copy(
            src_ref=own.at[slot] if hop == 1 else up_p.at[hop - 2, slot],
            dst_ref=up_p.at[hop - 1, slot],
            send_sem=p_send.at[0, hop - 1, slot],
            recv_sem=p_recv.at[0, hop - 1, slot],
            device_id=right,
            device_id_type=MESH,
        )

    def p_left(hop, slot):
        return pltpu.make_async_remote_copy(
            src_ref=own.at[slot] if hop == 1 else down_p.at[hop - 2, slot],
            dst_ref=down_p.at[hop - 1, slot],
            send_sem=p_send.at[1, hop - 1, slot],
            recv_sem=p_recv.at[1, hop - 1, slot],
            device_id=left,
            device_id_type=MESH,
        )

    def s_right(hop, slot):
        return pltpu.make_async_remote_copy(
            src_ref=square.at[slot] if hop == 1 else up_s.at[hop - 2, slot],
            dst_ref=up_s.at[hop - 1, slot],
            send_sem=s_send.at[0, hop - 1, slot],
            recv_sem=s_recv.at[0, hop - 1, slot],
            device_id=right,
            device_id_type=MESH,
        )

    def s_left(hop, slot):
        return pltpu.make_async_remote_copy(
            src_ref=square.at[slot] if hop == 1 else down_s.at[hop - 2, slot],
            dst_ref=down_s.at[hop - 1, slot],
            send_sem=s_send.at[1, hop - 1, slot],
            recv_sem=s_recv.at[1, hop - 1, slot],
            device_id=left,
            device_id_type=MESH,
        )

    barrier = pltpu.get_barrier_semaphore()
    for neighbour in (left, right):
        pl.semaphore_signal(barrier, inc=1, device_id=neighbour, device_id_type=MESH)

    @pl.when(moved)
    def _():
        for partner in (worker, owner):
            pl.semaphore_signal(barrier, inc=1, device_id=partner, device_id_type=MESH)

    for slot in range(SLOTS):
        column = lax.rem(given_row + slot, total)
        listed = jnp.int32(0)
        for entry in range(pattern.shape[1]):
            listed = listed | (pattern[0, entry] == column).astype(jnp.int32)
        given_flags[slot : slot + 1, :] = jnp.full((1, 128), listed.astype(jnp.float32))
    given_flags[SLOTS:, :] = jnp.zeros((1, 128), jnp.float32)

    @pl.when(moved)
    def _():
        pl.semaphore_wait(barrier, 4)
        for slot in FAR_FIRST:
            move_in(slot).start()
        move_flags().start()

    @pl.when(jnp.logical_not(moved))
    def _():
        for slot in range(SLOTS):
            own[slot] = given[0, slot]
        flags[...] = given_flags[...]
        pl.semaphore_wait(barrier, 2)

    for slot in FAR_FIRST:

        @pl.when(moved)
        def _():
            move_in(slot).wait_recv()

        if slot >= 1:
            p_right(1, slot).start()
        if slot < REACH:
            p_left(1, slot).start()

    @pl.when(moved)
    def _():
        move_flags().wait_recv()

    for slot in range(SLOTS):
        high, low = split(own[slot])
        own_high[slot] = high
        own_low[slot] = low

    def own_pair(first, last):
        return (
            side([own_high[i] for i in range(first, last)]),
            side([own_low[i] for i in range(first, last)]),
        )

    def add(target, first, value):
        for i in range(value.shape[1] // 128):
            target[first + i] += value[:, i * 128 : (i + 1) * 128]

    def local(target, band_high_low):
        band = band_high_low
        value = times(own_pair(0, 1), band)
        for i in range(SLOTS):
            target[i] = value[:, i * 128 : (i + 1) * 128]
        rest = (band[0][:, 128:], band[1][:, 128:])
        target[0] += times_transposed(own_pair(1, SLOTS), rest)

    def from_up(target, buffer, hop):
        value = split(side([buffer[hop - 1, i] for i in range(hop, SLOTS)]))
        add(target, 0, times((left_high[hop - 1], left_low[hop - 1]), value))

    def from_down(target, buffer, hop):
        value = split(side([buffer[hop - 1, i] for i in range(SLOTS - hop)]))
        add(target, hop, times(own_pair(hop, hop + 1), value))
        if hop < REACH:
            rest = (value[0][:, 128:], value[1][:, 128:])
            add(target, hop, times_transposed(own_pair(hop + 1, SLOTS), rest))

    local(square, own_pair(0, SLOTS))

    for step in range(1, 2 * REACH + 1):
        if step <= REACH:
            for slot in range(SLOTS - step):
                p_right(step, REACH - slot).wait_recv()
                if REACH - slot > step:
                    p_right(step + 1, REACH - slot).start()
                p_left(step, slot).wait_recv()
                if slot < REACH - step:
                    p_left(step + 1, slot).start()
        for hop in range(REACH, 0, -1):
            for slot in range(SLOTS):
                if ready(slot) + hop != step:
                    continue
                if hop <= slot:
                    s_right(hop, slot).wait_recv()
                    if hop < slot:
                        s_right(hop + 1, slot).start()
                if hop <= REACH - slot:
                    s_left(hop, slot).wait_recv()
                    if hop < REACH - slot:
                        s_left(hop + 1, slot).start()
        if step <= REACH:
            high, low = split(up_p[step - 1, step].T)
            left_high[step - 1] = high
            left_low[step - 1] = low
            from_up(square, up_p, step)
            from_down(square, down_p, step)
            for slot in range(SLOTS):
                if ready(slot) == step:
                    square[slot] = square[slot] * flags[slot : slot + 1, :]
                    if slot >= 1:
                        s_right(1, slot).start()
                    if slot < REACH:
                        s_left(1, slot).start()
            if step == REACH:
                local(cube, split(side([square[i] for i in range(SLOTS)])))
        else:
            from_up(cube, up_s, step - REACH)
            from_down(cube, down_s, step - REACH)
            for slot in range(SLOTS):
                if ready(slot) == step - REACH:
                    twice = 2.0 * flags[slot : slot + 1, :]
                    result[slot] = 3.0 * square[slot] - twice * cube[slot]

                    @pl.when(moved)
                    def _():
                        move_out(slot).start()

                    @pl.when(jnp.logical_not(moved))
                    def _():
                        out[0, slot] = result[slot]

    for hop in range(1, REACH + 1):
        for slot in range(SLOTS):
            if hop <= slot:
                p_right(hop, slot).wait_send()
                s_right(hop, slot).wait_send()
            if hop <= REACH - slot:
                p_left(hop, slot).wait_send()
                s_left(hop, slot).wait_send()

    @pl.when(moved)
    def _():
        move_flags().wait_send()
        for slot in range(SLOTS):
            move_in(slot).wait_send()
            move_out(slot).wait()


def solution(mesh):
    rows, cols = mesh.shape["row"], mesh.shape["col"]

    def on_device(density, pattern):
        halo = pltpu.VMEM((REACH, SLOTS, 128, 128), jnp.float32)
        band = pltpu.VMEM((SLOTS, 128, 128), jnp.float32)
        return pl.pallas_call(
            functools.partial(kernel, rows, cols),
            out_shape=jax.ShapeDtypeStruct(density.shape, jnp.float32),
            in_specs=[
                pl.BlockSpec(memory_space=pltpu.VMEM),
                pl.BlockSpec(memory_space=pltpu.SMEM),
            ],
            out_specs=pl.BlockSpec(memory_space=pltpu.VMEM),
            scratch_shapes=[
                band,
                band,
                pltpu.VMEM((SLOTS + 1, 128), jnp.float32),
                pltpu.VMEM((SLOTS + 1, 128), jnp.float32),
                halo,
                halo,
                halo,
                halo,
                band,
                band,
                pltpu.VMEM((SLOTS, 128, 128), jnp.bfloat16),
                pltpu.VMEM((SLOTS, 128, 128), jnp.bfloat16),
                pltpu.VMEM((REACH, 128, 128), jnp.bfloat16),
                pltpu.VMEM((REACH, 128, 128), jnp.bfloat16),
                pltpu.SemaphoreType.DMA((2, REACH, SLOTS)),
                pltpu.SemaphoreType.DMA((2, REACH, SLOTS)),
                pltpu.SemaphoreType.DMA((2, REACH, SLOTS)),
                pltpu.SemaphoreType.DMA((2, REACH, SLOTS)),
                pltpu.SemaphoreType.DMA((2, SLOTS + 1)),
                pltpu.SemaphoreType.DMA((2, SLOTS + 1)),
            ],
            compiler_params=pltpu.CompilerParams(
                collective_id=0, has_side_effects=True, vmem_limit_bytes=40 * 1024 * 1024
            ),
            cost_estimate=pl.CostEstimate(
                flops=140 * 2 * 128**3, bytes_accessed=14 * 4 * 128**2, transcendentals=0
            ),
        )(density, pattern)

    return jax.shard_map(
        on_device,
        mesh=mesh,
        in_specs=(P(("row", "col"), None, None, None), P(("row", "col"), None)),
        out_specs=P(("row", "col"), None, None, None),
        check_vma=False,
    )
```

```python
import functools

import jax
import jax.numpy as jnp
from jax import lax
from jax.experimental import pallas as pl
from jax.experimental.pallas import tpu as pltpu
from jax.sharding import PartitionSpec as P

REACH = 6
SLOTS = REACH + 1
MESH = pl.DeviceIdType.MESH
FAR_FIRST = (3, 2, 4, 1, 5, 0, 6)
NN = (((1,), (0,)), ((), ()))
NT = (((1,), (1,)), ((), ()))


def split(value):
    high = value.astype(jnp.bfloat16)
    low = (value - high.astype(jnp.float32)).astype(jnp.bfloat16)
    return high, low


def side(blocks):
    return blocks[0] if len(blocks) == 1 else jnp.concatenate(blocks, axis=1)


def times(left, right):
    lh, ll = left
    rh, rl = right
    return lax.dot_general(
        jnp.concatenate([lh, ll, lh], axis=1),
        jnp.concatenate([rh, rh, rl], axis=0),
        NN,
        preferred_element_type=jnp.float32,
    )


def times_transposed(left, right):
    lh, ll = left
    rh, rl = right
    return lax.dot_general(
        jnp.concatenate([lh, ll, lh], axis=1),
        jnp.concatenate([rh, rh, rl], axis=1),
        NT,
        preferred_element_type=jnp.float32,
    )


def ready(slot):
    return max(slot, REACH - slot)


CYCLE = (0, 8, 9, 1, 5, 6, 7, 3, 2, 10, 11, 15, 14, 13, 12, 4)


def look_up(table, index):
    value = jnp.int32(0)
    for place, entry in enumerate(table):
        value = value + jnp.where(index == place, entry, 0)
    return value


def cycle_device(rows, cols, index):
    if (rows, cols) == (4, 8):
        index = 2 * look_up(CYCLE, index // 2) + lax.rem(index, 2)
    return index // cols, lax.rem(index, cols)


def cycle_row(rows, cols, line, place):
    index = line * cols + place
    if (rows, cols) == (4, 8):
        chips = [CYCLE.index(chip) for chip in range(len(CYCLE))]
        index = 2 * look_up(chips, index // 2) + lax.rem(index, 2)
    return index


def kernel(
    rows,
    cols,
    given,
    pattern,
    out,
    own,
    result,
    given_flags,
    flags,
    up_p,
    down_p,
    up_s,
    down_s,
    square,
    cube,
    own_high,
    own_low,
    left_high,
    left_low,
    p_send,
    p_recv,
    s_send,
    s_recv,
    swap_send,
    swap_recv,
):
    total = rows * cols
    line, place = lax.axis_index("row"), lax.axis_index("col")
    given_row = line * cols + place
    me = cycle_row(rows, cols, line, place)

    def device(index):
        return cycle_device(rows, cols, index)

    right = device(lax.rem(me + 1, total))
    left = device(lax.rem(me + total - 1, total))
    worker = device(given_row)
    owner = (me // cols, lax.rem(me, cols))
    moved = me != given_row

    def move(source, target, kind, index, to):
        return pltpu.make_async_remote_copy(
            src_ref=source,
            dst_ref=target,
            send_sem=swap_send.at[kind, index],
            recv_sem=swap_recv.at[kind, index],
            device_id=to,
            device_id_type=MESH,
        )

    def move_in(slot):
        return move(given.at[0, slot], own.at[slot], 0, slot, worker)

    def move_flags():
        return move(given_flags, flags, 0, SLOTS, worker)

    def move_out(slot):
        return move(result.at[slot], out.at[0, slot], 1, slot, owner)

    def p_right(hop, slot):
        return pltpu.make_async_remote_copy(
            src_ref=own.at[slot] if hop == 1 else up_p.at[hop - 2, slot],
            dst_ref=up_p.at[hop - 1, slot],
            send_sem=p_send.at[0, hop - 1, slot],
            recv_sem=p_recv.at[0, hop - 1, slot],
            device_id=right,
            device_id_type=MESH,
        )

    def p_left(hop, slot):
        return pltpu.make_async_remote_copy(
            src_ref=own.at[slot] if hop == 1 else down_p.at[hop - 2, slot],
            dst_ref=down_p.at[hop - 1, slot],
            send_sem=p_send.at[1, hop - 1, slot],
            recv_sem=p_recv.at[1, hop - 1, slot],
            device_id=left,
            device_id_type=MESH,
        )

    def s_right(hop, slot):
        return pltpu.make_async_remote_copy(
            src_ref=square.at[slot] if hop == 1 else up_s.at[hop - 2, slot],
            dst_ref=up_s.at[hop - 1, slot],
            send_sem=s_send.at[0, hop - 1, slot],
            recv_sem=s_recv.at[0, hop - 1, slot],
            device_id=right,
            device_id_type=MESH,
        )

    def s_left(hop, slot):
        return pltpu.make_async_remote_copy(
            src_ref=square.at[slot] if hop == 1 else down_s.at[hop - 2, slot],
            dst_ref=down_s.at[hop - 1, slot],
            send_sem=s_send.at[1, hop - 1, slot],
            recv_sem=s_recv.at[1, hop - 1, slot],
            device_id=left,
            device_id_type=MESH,
        )

    barrier = pltpu.get_barrier_semaphore()
    for neighbour in (left, right):
        pl.semaphore_signal(barrier, inc=1, device_id=neighbour, device_id_type=MESH)

    @pl.when(moved)
    def _():
        for partner in (worker, owner):
            pl.semaphore_signal(barrier, inc=1, device_id=partner, device_id_type=MESH)

    for slot in range(SLOTS):
        column = lax.rem(given_row + slot, total)
        listed = jnp.int32(0)
        for entry in range(pattern.shape[1]):
            listed = listed | (pattern[0, entry] == column).astype(jnp.int32)
        given_flags[slot : slot + 1, :] = jnp.full((1, 128), listed.astype(jnp.float32))
    given_flags[SLOTS:, :] = jnp.zeros((1, 128), jnp.float32)

    @pl.when(moved)
    def _():
        pl.semaphore_wait(barrier, 4)
        for slot in FAR_FIRST:
            move_in(slot).start()
        move_flags().start()

    @pl.when(jnp.logical_not(moved))
    def _():
        for slot in range(SLOTS):
            own[slot] = given[0, slot]
        flags[...] = given_flags[...]
        pl.semaphore_wait(barrier, 2)

    for slot in FAR_FIRST:

        @pl.when(moved)
        def _():
            move_in(slot).wait_recv()

        if slot >= 1:
            p_right(1, slot).start()
        if slot < REACH:
            p_left(1, slot).start()

    @pl.when(moved)
    def _():
        move_flags().wait_recv()

    for slot in range(SLOTS):
        high, low = split(own[slot])
        own_high[slot] = high
        own_low[slot] = low

    def own_pair(first, last):
        return (
            side([own_high[i] for i in range(first, last)]),
            side([own_low[i] for i in range(first, last)]),
        )

    def add(target, first, value):
        for i in range(value.shape[1] // 128):
            target[first + i] += value[:, i * 128 : (i + 1) * 128]

    def local(target, band_high_low):
        band = band_high_low
        value = times(own_pair(0, 1), band)
        for i in range(SLOTS):
            target[i] = value[:, i * 128 : (i + 1) * 128]
        rest = (band[0][:, 128:], band[1][:, 128:])
        target[0] += times_transposed(own_pair(1, SLOTS), rest)

    def from_up(target, buffer, hop):
        value = split(side([buffer[hop - 1, i] for i in range(hop, SLOTS)]))
        add(target, 0, times((left_high[hop - 1], left_low[hop - 1]), value))

    def from_down(target, buffer, hop):
        value = split(side([buffer[hop - 1, i] for i in range(SLOTS - hop)]))
        add(target, hop, times(own_pair(hop, hop + 1), value))
        if hop < REACH:
            rest = (value[0][:, 128:], value[1][:, 128:])
            add(target, hop, times_transposed(own_pair(hop + 1, SLOTS), rest))

    local(square, own_pair(0, SLOTS))

    for step in range(1, 2 * REACH + 1):
        if step <= REACH:
            for slot in range(SLOTS - step):
                p_right(step, REACH - slot).wait_recv()
                if REACH - slot > step:
                    p_right(step + 1, REACH - slot).start()
                p_left(step, slot).wait_recv()
                if slot < REACH - step:
                    p_left(step + 1, slot).start()
        for hop in range(REACH, 0, -1):
            for slot in range(SLOTS):
                if ready(slot) + hop != step:
                    continue
                if hop <= slot:
                    s_right(hop, slot).wait_recv()
                    if hop < slot:
                        s_right(hop + 1, slot).start()
                if hop <= REACH - slot:
                    s_left(hop, slot).wait_recv()
                    if hop < REACH - slot:
                        s_left(hop + 1, slot).start()
        if step <= REACH:
            high, low = split(up_p[step - 1, step].T)
            left_high[step - 1] = high
            left_low[step - 1] = low
            from_up(square, up_p, step)
            from_down(square, down_p, step)
            for slot in range(SLOTS):
                if ready(slot) == step:
                    square[slot] = square[slot] * flags[slot : slot + 1, :]
                    if slot >= 1:
                        s_right(1, slot).start()
                    if slot < REACH:
                        s_left(1, slot).start()
            if step == REACH:
                local(cube, split(side([square[i] for i in range(SLOTS)])))
        else:
            from_up(cube, up_s, step - REACH)
            from_down(cube, down_s, step - REACH)
            for slot in range(SLOTS):
                if ready(slot) == step - REACH:
                    twice = 2.0 * flags[slot : slot + 1, :]
                    result[slot] = 3.0 * square[slot] - twice * cube[slot]

                    @pl.when(moved)
                    def _():
                        move_out(slot).start()

                    @pl.when(jnp.logical_not(moved))
                    def _():
                        out[0, slot] = result[slot]

    for hop in range(1, REACH + 1):
        for slot in range(SLOTS):
            if hop <= slot:
                p_right(hop, slot).wait_send()
                s_right(hop, slot).wait_send()
            if hop <= REACH - slot:
                p_left(hop, slot).wait_send()
                s_left(hop, slot).wait_send()

    @pl.when(moved)
    def _():
        move_flags().wait_send()
        for slot in range(SLOTS):
            move_in(slot).wait_send()
            move_out(slot).wait()


def solution(mesh):
    rows, cols = mesh.shape["row"], mesh.shape["col"]

    def on_device(density, pattern):
        halo = pltpu.VMEM((REACH, SLOTS, 128, 128), jnp.float32)
        band = pltpu.VMEM((SLOTS, 128, 128), jnp.float32)
        return pl.pallas_call(
            functools.partial(kernel, rows, cols),
            out_shape=jax.ShapeDtypeStruct(density.shape, jnp.float32),
            in_specs=[
                pl.BlockSpec(memory_space=pltpu.VMEM),
                pl.BlockSpec(memory_space=pltpu.SMEM),
            ],
            out_specs=pl.BlockSpec(memory_space=pltpu.VMEM),
            scratch_shapes=[
                band,
                band,
                pltpu.VMEM((SLOTS + 1, 128), jnp.float32),
                pltpu.VMEM((SLOTS + 1, 128), jnp.float32),
                halo,
                halo,
                halo,
                halo,
                band,
                band,
                pltpu.VMEM((SLOTS, 128, 128), jnp.bfloat16),
                pltpu.VMEM((SLOTS, 128, 128), jnp.bfloat16),
                pltpu.VMEM((REACH, 128, 128), jnp.bfloat16),
                pltpu.VMEM((REACH, 128, 128), jnp.bfloat16),
                pltpu.SemaphoreType.DMA((2, REACH, SLOTS)),
                pltpu.SemaphoreType.DMA((2, REACH, SLOTS)),
                pltpu.SemaphoreType.DMA((2, REACH, SLOTS)),
                pltpu.SemaphoreType.DMA((2, REACH, SLOTS)),
                pltpu.SemaphoreType.DMA((2, SLOTS + 1)),
                pltpu.SemaphoreType.DMA((2, SLOTS + 1)),
            ],
            compiler_params=pltpu.CompilerParams(
                collective_id=0, has_side_effects=True, vmem_limit_bytes=40 * 1024 * 1024
            ),
            cost_estimate=pl.CostEstimate(
                flops=140 * 2 * 128**3, bytes_accessed=14 * 4 * 128**2, transcendentals=0
            ),
        )(density, pattern)

    return jax.shard_map(
        on_device,
        mesh=mesh,
        in_specs=(P(("row", "col"), None, None, None), P(("row", "col"), None)),
        out_specs=P(("row", "col"), None, None, None),
        check_vma=False,
    )
```
